32 devices in a mesh: dp: 8 (over z, y), expert: 4 (over x, core).
Axes of the slice: x: 2, y: 2, z: 4, core: 2. Of those that a mesh axis runs over, the one named last changes fastest.
Arguments:
- tokens: bfloat16 [16384, 768], P(('dp', 'expert')), may hold values from -6 to 6
- segment_ids: int32 [32, 512], P(('dp', 'expert')), may hold values from 0 to 5, never falling along the last dimension, each value on 1 to 256 neighbouring positions
- expert_ids: int32 [16384, 2], P(('dp', 'expert')), may hold values from 0 to 7, all different within a row
- upstream: bfloat16 [16384, 768], P(('dp', 'expert')), may hold values from -6 to 6
- norm_first: bfloat16 [768], P(('dp', 'expert')), may hold values from 0.5 to 1.5
- qkv_weight: bfloat16 [768, 2304], P(('dp', 'expert')), may hold values from -0.21875 to 0.21875
- out_weight: bfloat16 [768, 768], P(('dp', 'expert')), may hold values from -0.625 to 0.625
- norm_second: bfloat16 [768], P(('dp', 'expert')), may hold values from 0.5 to 1.5
- router_weight: bfloat16 [768, 8], P(('dp', 'expert')), may hold values from -0.15625 to 0.15625
- shared_gate_up: bfloat16 [768, 4096], P(('dp', 'expert')), may hold values from -0.21875 to 0.21875
- shared_down: bfloat16 [2048, 768], P(('dp', 'expert')), may hold values from -0.1875 to 0.1875
- expert_gate_up: bfloat16 [8, 768, 4096], P('expert', 'dp'), may hold values from -0.21875 to 0.21875
- expert_down: bfloat16 [8, 2048, 768], P('expert', 'dp'), may hold values from -0.1875 to 0.1875
Outputs:
- mixed: bfloat16 [16384, 768], P(('dp', 'expert'))
- input_grad: float32 [16384, 768], P(('dp', 'expert'))
- norm_first_grad: float32 [768], P(('dp', 'expert'))
- qkv_grad: float32 [768, 2304], P(('dp', 'expert'))
- out_weight_grad: float32 [768, 768], P(('dp', 'expert'))
- norm_second_grad: float32 [768], P(('dp', 'expert'))
- router_grad: float32 [768, 8], P(('dp', 'expert'))
- shared_gate_up_grad: float32 [768, 4096], P(('dp', 'expert'))
- shared_down_grad: float32 [2048, 768], P(('dp', 'expert'))
- expert_gate_up_grad: float32 [8, 768, 4096], P('expert', 'dp')
- expert_down_grad: float32 [8, 2048, 768], P('expert', 'dp')
The draws below stay inside these ranges and needn't reach their ends.
Inputs may be any that keep to these rules, and one draw needn't show every extreme that they name: `expert_ids`: each token names two different experts. `segment_ids`: segment numbers never fall along a sequence, and each of the 6 numbers appears in every sequence.
All inputs are finite; a program needn't handle non-finite values.
Results may differ from the reference program's by a relative error of at most 0.015.
Values may be sent and summed in bfloat16 or wider, within the bound.
No kernel may reach another device: no remote copies, remote signals or barrier semaphores. Data moves between devices by JAX's collectives and lax.ppermute only.
A program may use at most 256 MiB of HBM per device.

```python
import math
import jax
import jax.numpy as jnp
import numpy as np
from jax import lax

D = 768
HEADS = 12
HEAD_DIM = 64
FF = 2048
FS = 2048
TOP = 2
DOCS = 6
TOK_DEV = 512
EXPERTS = 8
CAP = 128
SEQS = 32
TOKENS = 16384


def steps_of(stream_key, extent, split, low, top_value):
    def one(axis_at, blocks):
        steps = jax.random.uniform(jax.random.fold_in(jax.random.fold_in(stream_key, 6), axis_at), (blocks,), jnp.float32, low / len(split), top_value / len(split))
        return jnp.repeat(jnp.exp(steps), extent[axis_at] // blocks).reshape((-1,) + (1,) * (len(extent) - axis_at - 1))

    level = one(*split[0])
    for cut in split[1:]:
        level = level * one(*cut)
    return level


def distinct(stream_key, rows, amount, top, lift):
    order = jax.random.permutation(jax.random.fold_in(stream_key, 1), amount)
    boost = order
    for power in range(3):
        boost = boost * boost // amount
    boost = boost * lift // amount
    lots = jax.random.randint(jax.random.fold_in(stream_key, 2), (rows, amount), 0, 4096) + boost
    holders = jax.random.permutation(jax.random.fold_in(stream_key, 3), rows)[jnp.arange(amount) % rows]
    lots = jnp.where(jnp.arange(rows)[:, None] == holders[None, :], 1 << 14, lots)
    score = lots * amount + jnp.arange(amount)
    return lax.top_k(score.astype(jnp.int32), top)[1].astype(jnp.int32)


def length_profile(amount, total, most, skew):
    portions = [(1 << 20) // math.isqrt(rank ** skew) + 1 for rank in range(2, amount + 1)]
    rest, given = total - most - (amount - 1), [1] * (amount - 1)
    while rest > 0:
        candidates = [i for i in range(amount - 1) if given[i] < most]
        whole, remaining = sum([portions[i] for i in candidates]), rest
        for i in candidates:
            more = min(most - given[i], max(1, remaining * portions[i] // whole), rest)
            given[i] = given[i] + more
            rest = rest - more
    return np.array([most] + given)


def uneven_parts(key, number_of, total, limit, lean):
    if number_of == 2:
        one = jax.random.randint(key, (), max(1, total - limit), min(limit, total - 1) + 1)
        return jnp.stack([one, total - one])
    tallies = jnp.asarray(length_profile(number_of, total, limit, lean), jnp.int32)
    twos = (number_of - 1) // 2
    donor, sink = tallies[1:1 + 2 * twos:2], tallies[2:2 + 2 * twos:2]
    room = jnp.minimum(donor - 1, limit - sink)
    moved = jax.random.randint(jax.random.fold_in(key, 1), (twos,), 0, 1 << 20) % (room + 1)
    tallies = tallies.at[1:1 + 2 * twos:2].set(donor - moved).at[2:2 + 2 * twos:2].set(sink + moved)
    return tallies[jax.random.permutation(jax.random.fold_in(key, 2), number_of)]


def gaussian(rng, shape, width, most, split=(), kind=jnp.bfloat16):
    entries = jax.random.normal(rng, shape, jnp.float32) * width
    if len(split) > 0:
        entries = steps_of(rng, shape, split, -0.22, 0.18) * entries
    return jnp.clip(entries, min=-most, max=most).astype(kind)


def setup_inputs(seed: int = 0) -> dict:
    splits = jax.random.split(jax.random.key(seed), 14)
    return {
        "tokens": gaussian(splits[0], (TOKENS, D), 1.0, 6.0, ((0, 32),)),
        "segment_ids": jax.vmap(lambda own: jnp.searchsorted(jnp.cumsum(uneven_parts(own, DOCS, TOK_DEV, TOK_DEV // 2, 2)), jnp.arange(TOK_DEV), side="right"))(jax.random.split(splits[1], SEQS)).reshape((SEQS, TOK_DEV)).astype(jnp.int32),
        "expert_ids": distinct(splits[2], TOKENS, EXPERTS, TOP, 2048),
        "upstream": gaussian(splits[3], (TOKENS, D), 1.0, 6.0, ((0, 32),)),
        "norm_first": jnp.clip(1.0 + 0.1 * jax.random.normal(splits[4], (D,), jnp.float32), 0.5, 1.5).astype(jnp.bfloat16),
        "qkv_weight": gaussian(splits[5], (D, 3 * D), D ** -0.5, 0.21875, ((0, 32),)),
        "out_weight": gaussian(splits[6], (D, D), (D // 8) ** -0.5, 0.625, ((0, 32),)),
        "norm_second": jnp.clip(1.0 + 0.1 * jax.random.normal(splits[7], (D,), jnp.float32), 0.5, 1.5).astype(jnp.bfloat16),
        "router_weight": gaussian(splits[8], (D, EXPERTS), (2 * D) ** -0.5, 0.15625, ((0, 32),)),
        "shared_gate_up": gaussian(splits[9], (D, 2 * FS), D ** -0.5, 0.21875, ((0, 32),)),
        "shared_down": gaussian(splits[10], (FS, D), (FS // 2) ** -0.5, 0.1875, ((0, 32),)),
        "expert_gate_up": gaussian(splits[11], (EXPERTS, D, 2 * FF), D ** -0.5, 0.21875, ((0, 4), (1, 8))),
        "expert_down": gaussian(splits[12], (EXPERTS, FF, D), (FF // 2) ** -0.5, 0.1875, ((0, 4), (1, 8))),
    }


epsilon = 1e-06
highest = lax.Precision.HIGHEST

@jax.custom_vjp
def low(v):
    return lax.optimization_barrier(v.astype(jnp.bfloat16)).astype(jnp.float32)

@jax.custom_vjp
def low_back(v):
    return v

def low_keep(v):
    return (low(v), None)

def low_pass(kept, grad):
    return (grad,)

def back_keep(v):
    return (v, None)

def back_low(kept, grad):
    return (low(grad),)
low.defvjp(low_keep, low_pass)
low_back.defvjp(back_keep, back_low)

def matmul_high(left, right):
    return jnp.dot(left, right, precision=highest, preferred_element_type=jnp.float32)

def rope_tables(length, head_width):
    half_width = head_width // 2
    frequency = 10000.0 ** (-jnp.arange(half_width, dtype=jnp.float32) / half_width)
    angles = jnp.arange(length, dtype=jnp.float32)[:, None] * frequency[None, :]
    angles = jnp.concatenate([angles, angles], axis=-1)[:, None, :]
    return (jnp.cos(angles), jnp.sin(angles))

def rotate(values, cosine_table, sine_table):
    half_width = values.shape[-1] // 2
    turned = jnp.concatenate([-values[..., half_width:], values[..., :half_width]], axis=-1)
    return values * cosine_table + turned * sine_table

def slot_table(expert_ids, experts, capacity):
    flat_ids = expert_ids.reshape(-1)
    one_hot = (flat_ids[:, None] == jnp.arange(experts, dtype=jnp.int32)[None, :]).astype(jnp.int32)
    earlier = jnp.cumsum(one_hot, axis=0) - one_hot
    slot_rank = lax.optimization_barrier(jnp.sum(earlier * one_hot, axis=1)).reshape(expert_ids.shape)
    kept_mask = slot_rank < capacity
    slot_index = jnp.where(kept_mask, expert_ids * capacity + slot_rank, experts * capacity)
    return (kept_mask, slot_index.astype(jnp.int32))

def layer_block(weights, stream, segments, expert_ids):
    gain_one, qkv_weight, out_weight, gain_two, router_weight, shared_gate_up, shared_down, expert_gate_up, expert_down = weights
    length = stream.shape[0]
    scale_one = lax.rsqrt(lax.optimization_barrier(jnp.mean(stream * stream, axis=-1, keepdims=True)) + epsilon)
    normed_low = low(stream * scale_one * gain_one)
    projected = matmul_high(normed_low, qkv_weight)
    cosine_table, sine_table = rope_tables(length, HEAD_DIM)
    query_rot = low(rotate(low_back(projected[:, :D]).reshape(length, HEADS, HEAD_DIM), cosine_table, sine_table))
    key_rot = low(rotate(low_back(projected[:, D:2 * D]).reshape(length, HEADS, HEAD_DIM), cosine_table, sine_table))
    value_low = low(low_back(projected[:, 2 * D:])).reshape(length, HEADS, HEAD_DIM)
    position = jnp.arange(length)
    allowed = (position[:, None] >= position[None, :]) & (segments[:, None] == segments[None, :])
    scores = low_back(jnp.einsum('qhd,khd->hqk', query_rot, key_rot, precision=highest) * HEAD_DIM ** (-0.5))
    scores = jnp.where(allowed[None], scores, -1000000000.0)
    top_score = lax.optimization_barrier(jnp.max(scores, axis=-1, keepdims=True))
    exp_scores = jnp.exp(scores - top_score)
    attn_probs = exp_scores / lax.optimization_barrier(jnp.sum(exp_scores, axis=-1, keepdims=True))
    attended = jnp.einsum('hqk,khd->qhd', low(attn_probs), value_low, precision=highest).reshape(length, D)
    attended = low(low_back(attended))
    stream_mid = stream + low_back(matmul_high(attended, out_weight))
    scale_two = lax.rsqrt(lax.optimization_barrier(jnp.mean(stream_mid * stream_mid, axis=-1, keepdims=True)) + epsilon)
    expert_in = low(stream_mid * scale_two * gain_two)
    logits = low_back(matmul_high(expert_in, router_weight))
    chosen = jnp.take_along_axis(logits, expert_ids, axis=1)
    chosen_top = lax.optimization_barrier(jnp.max(chosen, axis=1, keepdims=True))
    chosen_exp = jnp.exp(chosen - chosen_top)
    gate_values = chosen_exp / lax.optimization_barrier(jnp.sum(chosen_exp, axis=1, keepdims=True))
    shared_pre = low_back(matmul_high(expert_in, shared_gate_up))
    shared_hidden = low(jax.nn.silu(shared_pre[:, :FS]) * shared_pre[:, FS:])
    shared_out = matmul_high(shared_hidden, shared_down)
    kept_mask, slot_index = slot_table(expert_ids, EXPERTS, CAP)
    repeated = jnp.broadcast_to(expert_in[:, None, :], (length, 2, D)).reshape(length * 2, D)
    buffer = jnp.zeros((EXPERTS * CAP + 1, D), jnp.float32).at[slot_index.reshape(-1)].add(repeated)
    buffer = low_back(buffer[:EXPERTS * CAP].reshape(EXPERTS, CAP, D))
    expert_pre = low_back(jnp.einsum('ecd,edf->ecf', buffer, expert_gate_up, precision=highest))
    expert_hidden = low(jax.nn.silu(expert_pre[..., :FF]) * expert_pre[..., FF:])
    expert_out = low(low_back(jnp.einsum('ecf,efd->ecd', expert_hidden, expert_down, precision=highest)))
    padded = jnp.concatenate([expert_out.reshape(EXPERTS * CAP, D), jnp.zeros((1, D), jnp.float32)], axis=0)
    picked = padded[slot_index]
    mix_weight = jnp.where(kept_mask, gate_values, 0.0)
    routed = lax.optimization_barrier(jnp.sum(mix_weight[:, :, None] * picked, axis=1))
    return stream_mid + routed + shared_out

def reference(tokens, segment_ids, expert_ids, upstream, norm_first, qkv_weight, out_weight, norm_second, router_weight, shared_gate_up, shared_down, expert_gate_up, expert_down):
    weights = tuple((weight_arg.astype(jnp.float32) for weight_arg in (norm_first, qkv_weight, out_weight, norm_second, router_weight, shared_gate_up, shared_down, expert_gate_up, expert_down)))
    streams = tokens.astype(jnp.float32).reshape(SEQS, TOK_DEV, D)
    routes = expert_ids.reshape(SEQS, TOK_DEV, 2)
    checked = jax.checkpoint(layer_block)

    def forward(stream_all, weight_all):

        def one_step(carry, pieces):
            return (carry, checked(weight_all, pieces[0], pieces[1], pieces[2]))
        unused, outputs = lax.scan(one_step, jnp.zeros((), jnp.float32), (stream_all, segment_ids, routes))
        return outputs
    outputs, pullback = jax.vjp(forward, streams, weights)
    stream_grad, grads = pullback(upstream.astype(jnp.float32).reshape(SEQS, TOK_DEV, D))
    return (outputs.reshape(TOKENS, D).astype(jnp.bfloat16), stream_grad.reshape(TOKENS, D), grads[0], grads[1], grads[2], grads[3], grads[4], grads[5], grads[6], grads[7], grads[8])
```

```python
import functools

import jax
import jax.numpy as jnp
from jax import lax
from jax.experimental import pallas as pl
from jax.experimental.pallas import tpu as pltpu
from jax.sharding import PartitionSpec as P

D = 768
HEADS = 12
HEAD_DIM = 64
FF = 2048
CHUNK = 256
AX = ("dp", "expert")
PAIR_LOW = False

epsilon = 1e-06
bf16 = jnp.bfloat16
f32 = jnp.float32


def dot(left, right, left_dim, right_dim, precision=None):
    return lax.dot_general(
        left,
        right,
        (((left_dim,), (right_dim,)), ((), ())),
        preferred_element_type=f32,
        precision=precision,
    )


def rope_tables(length, head_width):
    half_width = head_width // 2
    frequency = 10000.0 ** (-jnp.arange(half_width, dtype=jnp.float32) / half_width)
    angles = jnp.arange(length, dtype=jnp.float32)[:, None] * frequency[None, :]
    angles = jnp.concatenate([angles, angles], axis=-1)[:, None, :]
    return (jnp.cos(angles), jnp.sin(angles))


def rotate(values, cosine_table, sine_table):
    half_width = values.shape[-1] // 2
    turned = jnp.concatenate([-values[..., half_width:], values[..., :half_width]], axis=-1)
    return values * cosine_table + turned * sine_table


def rotate_back(grads, cosine_table, sine_table):
    half_width = grads.shape[-1] // 2
    sined = grads * sine_table
    return grads * cosine_table + jnp.concatenate(
        [sined[..., half_width:], -sined[..., :half_width]], axis=-1
    )


def norm_back(grad_normed, normed, scale):
    return scale * (grad_normed - normed * jnp.mean(grad_normed * normed, axis=-1, keepdims=True))


def unpermute(values, order):
    high = values.astype(bf16)
    rest = (values - high.astype(f32)).astype(bf16)
    return dot(high, order, 1, 1) + dot(rest, order, 1, 1)


def two_layer_kernel(
    where_ref,
    a_ref,
    b_ref,
    x_ref,
    u_ref,
    w_ref,
    order_ref,
    gate_ref,
    up_ref,
    down_ref,
    *refs,
    routed,
    subs,
):
    if routed:
        out_ref, dx_ref, gg_ref, dgu_ref, dd_ref, xp, go, out_sum, dx_sum = refs
    else:
        out_ref, dx_ref, dgu_ref, dd_ref, xp, go, out_sum, dx_sum = refs
    step = pl.program_id(0)

    @pl.when(step == 0)
    def _():
        xp[...] = dot(x_ref[...], order_ref[...], 1, 0).astype(bf16)
        if routed:
            go[...] = (u_ref[...].astype(f32) * w_ref[...]).astype(bf16)
        else:
            go[...] = u_ref[...]

    x = xp[...]
    grad_out = go[...]
    cores, lanes = 2, subs // 2
    sub_x, sub_c = where_ref[0], where_ref[1]
    places = []
    for n in range(subs):
        places.append((lax.bitwise_xor(n % cores, sub_c), lax.bitwise_xor(n // cores, sub_x)))
    down = jnp.concatenate([down_ref[i, 0, j, 0] for i, j in places], axis=0)
    gate = dot(x, gate_ref[...], 1, 0)
    up = dot(x, up_ref[...], 1, 0)
    sigmoid = jax.nn.sigmoid(gate)
    act = gate * sigmoid
    slope = sigmoid * (1.0 + gate * (1.0 - sigmoid))
    hidden = (act * up).astype(bf16)
    out_part = dot(hidden, down, 1, 0)
    grad_hidden = dot(grad_out, down, 1, 1)
    grad_gate = (grad_hidden * up * slope).astype(bf16)
    grad_up = (grad_hidden * act).astype(bf16)
    dx_part = dot(grad_gate, gate_ref[...], 1, 1) + dot(grad_up, up_ref[...], 1, 1)
    grad_down = dot(hidden, grad_out, 0, 0).astype(bf16)
    rows = grad_down.shape[0] // subs
    for n, (i, j) in enumerate(places):
        dd_ref[i, 0, j, 0] = grad_down[n * rows : (n + 1) * rows]
    blocks, _, per, _ = dgu_ref.shape
    for half, grads in ((0, grad_gate), (1, grad_up)):
        weight_grad = dot(x, grads, 0, 0).astype(bf16)
        for n in range(blocks):
            dgu_ref[n, half] = weight_grad[n * per : (n + 1) * per]

    @pl.when(step == 0)
    def _():
        out_sum[...] = out_part
        dx_sum[...] = dx_part

    @pl.when(step > 0)
    def _():
        out_sum[...] += out_part
        dx_sum[...] += dx_part

    @pl.when(step == pl.num_programs(0) - 1)
    def _():
        if routed:
            out_low = out_sum[...].astype(bf16)
            out_ref[...] = out_low
            gg_ref[...] = jnp.sum(u_ref[...].astype(f32) * out_low.astype(f32), axis=1, keepdims=True)
            dx_ref[...] = dot(dx_sum[...].astype(bf16), order_ref[...], 1, 1).astype(bf16)
        else:
            out_ref[...] = out_sum[...]
            dx_ref[...] = unpermute(dx_sum[...], order_ref[...])


def two_layers(where, a_index, b_index, x, u, w, order, gate_up, down, blocks, routed):
    rows = x.shape[0]
    cores, a_size, lanes, b_size, per_down, _ = down.shape
    chunks = a_size * b_size
    width = FF // chunks
    per = D // blocks
    whole = lambda *shape: pl.BlockSpec(shape, lambda s, *_: (0,) * len(shape))
    down_spec = pl.BlockSpec(
        (cores, 1, lanes, 1, per_down, D), lambda s, q, a, b: (0, a[s], 0, b[s], 0, 0)
    )
    kind = bf16 if routed else f32
    outs = [
        jax.ShapeDtypeStruct((rows, D), kind),
        jax.ShapeDtypeStruct((rows, D), kind),
        jax.ShapeDtypeStruct((blocks, 2, per, FF), bf16),
        jax.ShapeDtypeStruct(down.shape, bf16),
    ]
    out_specs = [
        whole(rows, D),
        whole(rows, D),
        pl.BlockSpec((blocks, 2, per, width), lambda s, *_: (0, 0, 0, s)),
        down_spec,
    ]
    if routed:
        outs.insert(2, jax.ShapeDtypeStruct((rows, 1), f32))
        out_specs.insert(2, whole(rows, 1))
    return pl.pallas_call(
        functools.partial(two_layer_kernel, routed=routed, subs=cores * lanes),
        grid_spec=pltpu.PrefetchScalarGridSpec(
            num_scalar_prefetch=3,
            grid=(chunks,),
            in_specs=[
                whole(rows, D),
                whole(rows, D),
                whole(rows, 1),
                whole(D, D),
                pl.BlockSpec((D, width), lambda s, *_: (0, s)),
                pl.BlockSpec((D, width), lambda s, *_: (0, s + chunks)),
                down_spec,
            ],
            out_specs=out_specs,
            scratch_shapes=[
                pltpu.VMEM((rows, D), bf16),
                pltpu.VMEM((rows, D), bf16),
                pltpu.VMEM((rows, D), f32),
                pltpu.VMEM((rows, D), f32),
            ],
        ),
        out_shape=outs,
        compiler_params=pltpu.CompilerParams(vmem_limit_bytes=56 << 20),
        cost_estimate=pl.CostEstimate(
            flops=2 * 9 * rows * D * FF,
            bytes_accessed=12 * D * FF + 12 * rows * D,
            transcendentals=rows * FF,
        ),
        name="two_layers",
    )(where, a_index, b_index, x, u, w, order, gate_up, gate_up, down)


def body(
    dp_size,
    expert_size,
    tokens,
    segment_ids,
    expert_ids,
    upstream,
    norm_first,
    qkv_weight,
    out_weight,
    norm_second,
    router_weight,
    shared_gate_up,
    shared_down,
    expert_gate_up,
    expert_down,
):
    devices = dp_size * expert_size
    lanes = expert_size // 2
    length = tokens.shape[0]
    experts = expert_gate_up.shape[0] * expert_size
    held = expert_gate_up.shape[0]
    group = experts // lanes
    pairs = dp_size // group
    capacity = length * 2 // experts
    score_scale = HEAD_DIM ** (-0.5)
    tall = dp_size // 2

    me = lax.axis_index(AX).astype(jnp.int32)
    my_dp, my_expert = me // expert_size, me % expert_size
    my_x, my_c = my_expert // 2, my_expert % 2
    if PAIR_LOW:
        pair_of, group_of = (lambda d: d % pairs), (lambda d: d // pairs)
        dp_of = lambda p, g: g * pairs + p
    else:
        pair_of, group_of = (lambda d: d // group), (lambda d: d % group)
        dp_of = lambda p, g: p * group + g
    my_p, my_g = pair_of(my_dp), group_of(my_dp)

    def hop(values, offset):
        return lax.ppermute(values, AX, [(s, s ^ offset) for s in range(devices)])

    def spread(values, offsets):
        return jnp.stack([values] + [hop(values, o) for o in offsets[1:]])

    def collect(blocks, offsets):
        total = blocks[0].astype(f32)
        for i, o in enumerate(offsets[1:]):
            total = total + hop(blocks[i + 1], o).astype(f32)
        return total

    tall_offsets = [2 * i * expert_size for i in range(tall)]
    flat_offsets = [y * expert_size + 2 * x for y in range(2) for x in range(lanes)]
    pair_offsets = [dp_of(p, 0) * expert_size for p in range(pairs)]
    group_offsets = [dp_of(0, g) * expert_size for g in range(group)]
    owner_offsets = [dp_of(0, g) * expert_size + 2 * x for g in range(group) for x in range(lanes)]

    def gather_dense(shard):
        return spread(spread(spread(shard, tall_offsets), flat_offsets), [0, 1])

    def scatter_dense(grads):
        grads = collect(grads, [0, 1]).astype(bf16)
        grads = collect(grads, flat_offsets).astype(bf16)
        return collect(grads, tall_offsets)

    def dense_home(position):
        i, j, c = position % tall, position // tall % (2 * lanes), position // tall // (2 * lanes)
        offset = (2 * i + j // lanes) * expert_size + 2 * (j % lanes) + c
        return lax.bitwise_xor(me, offset)

    def gather_expert(shard):
        halves = shard.reshape(held, 2, shard.shape[1] // 2, shard.shape[2])
        mine = lax.dynamic_index_in_dim(halves, my_c, 1, keepdims=False)
        other = hop(lax.dynamic_index_in_dim(halves, 1 - my_c, 1, keepdims=False), 1)
        all_held = jnp.concatenate(
            [jnp.where(my_c == 0, mine, other), jnp.where(my_c == 0, other, mine)], axis=0
        )
        parts = [
            lax.dynamic_index_in_dim(all_held, lax.bitwise_xor(my_g, g), 0, keepdims=False)
            for g in range(group)
        ]
        parts = jnp.stack([parts[0]] + [hop(parts[g], group_offsets[g]) for g in range(1, group)])
        return spread(spread(parts, pair_offsets), [0, 1])

    def scatter_expert(grads):
        grads = collect(grads, [0, 1]).astype(bf16)
        grads = collect(grads, pair_offsets).astype(bf16)
        parts = jnp.stack([grads[0]] + [hop(grads[g], group_offsets[g]) for g in range(1, group)])
        keep = [
            lax.dynamic_index_in_dim(parts, lax.bitwise_xor(my_g, my_c * held + j), 0)
            for j in range(held)
        ]
        give = [
            lax.dynamic_index_in_dim(parts, lax.bitwise_xor(my_g, (1 - my_c) * held + j), 0)
            for j in range(held)
        ]
        keep = jnp.concatenate(keep, axis=0)
        take = hop(jnp.concatenate(give, axis=0), 1)
        return jnp.stack([jnp.where(my_c == 0, keep, take), jnp.where(my_c == 0, take, keep)], axis=1)

    def expert_home(position):
        g, p, c = position % group, position // group % pairs, position // group // pairs
        dp = dp_of(lax.bitwise_xor(my_p, p), lax.bitwise_xor(my_g, g))
        return dp * 2 + lax.bitwise_xor(my_c, c)

    def order_of(home, blocks, width=D):
        per = width // blocks
        column = jnp.arange(width, dtype=jnp.int32)
        source = home(column // per) * per + column % per
        return (jnp.arange(width, dtype=jnp.int32)[:, None] == source[None, :]).astype(bf16)

    def exchange(blocks):
        return [blocks[0]] + [
            hop(b, o) for b, o in zip(blocks[1:], owner_offsets[1:], strict=True)
        ]

    dense_order = order_of(dense_home, devices)
    expert_order = order_of(expert_home, 2 * dp_size)

    small = jnp.concatenate(
        [norm_first[:, None], norm_second[:, None], router_weight], axis=1
    )
    small = jnp.pad(small, ((0, 0), (0, 128 - small.shape[1])))
    qkv_full = gather_dense(jnp.concatenate([qkv_weight, small], axis=1)).reshape(D, 3 * D + 128)
    out_full = gather_dense(out_weight).reshape(D, D)
    shared_gu_full = gather_dense(shared_gate_up).reshape(D, 2 * FF)
    shared_down_full = gather_dense(shared_down)
    expert_gu_full = gather_expert(expert_gate_up).reshape(D, 2 * FF)
    expert_down_full = gather_expert(expert_down)

    columns = jnp.arange(experts, dtype=jnp.int32)
    pickers = [(expert_ids[:, j : j + 1] == columns[None, :]).astype(f32) for j in range(2)]
    position = jnp.arange(length)
    earlier = (position[:, None] > position[None, :]).astype(bf16)
    counts = dot(earlier, (pickers[0] + pickers[1]).astype(bf16), 1, 0)
    kept, places = [], []
    for j in range(2):
        rank = jnp.sum(counts * pickers[j], axis=1).astype(jnp.int32)
        ids = expert_ids[:, j]
        kept_mask = rank < capacity
        block = lax.bitwise_xor(ids % group, my_g) * lanes + lax.bitwise_xor(ids // group, my_x)
        slot = jnp.where(kept_mask, block * capacity + rank, -1)
        kept.append(kept_mask.astype(f32))
        places.append(
            (slot[:, None] == jnp.arange(experts * capacity, dtype=jnp.int32)[None, :]).astype(bf16)
        )
    both_places = places[0] + places[1]

    def send_rows(values):
        rows = dot(both_places, values, 0, 0).astype(bf16).reshape(experts, capacity, D)
        return jnp.concatenate(exchange([rows[k] for k in range(experts)]), axis=0)

    upstream_rows = send_rows(upstream)

    small_full = dot(qkv_full[:, 3 * D :], dense_order, 0, 1)
    gain_one, gain_two = small_full[0:1], small_full[1:2]
    router_full = small_full[2 : 2 + experts].astype(bf16)
    stream = tokens.astype(f32)
    scale_one = lax.rsqrt(jnp.mean(stream * stream, axis=-1, keepdims=True) + epsilon)
    normed_one = stream * scale_one
    normed_low = (normed_one * gain_one).astype(bf16)
    normed_low = dot(normed_low, dense_order, 1, 0).astype(bf16)
    projected = dot(normed_low, qkv_full[:, : 3 * D], 1, 0)
    cosine_table, sine_table = rope_tables(length, HEAD_DIM)
    query_rot = rotate(
        projected[:, :D].reshape(length, HEADS, HEAD_DIM), cosine_table, sine_table
    ).astype(bf16)
    key_rot = rotate(
        projected[:, D : 2 * D].reshape(length, HEADS, HEAD_DIM), cosine_table, sine_table
    ).astype(bf16)
    value_low = projected[:, 2 * D :].astype(bf16).reshape(length, HEADS, HEAD_DIM)
    query_heads = jnp.swapaxes(query_rot, 0, 1)
    key_heads = jnp.swapaxes(key_rot, 0, 1)
    value_heads = jnp.swapaxes(value_low, 0, 1)
    segments = segment_ids[0]
    allowed = (position[:, None] >= position[None, :]) & (segments[:, None] == segments[None, :])

    def head_scores(query_head, key_head):
        scores = dot(query_head, key_head, 1, 1) * score_scale
        return jnp.where(allowed, scores, -1000000000.0)

    def head_forward(parts):
        query_head, key_head, value_head = parts
        scores = head_scores(query_head, key_head)
        top_score = jnp.max(scores, axis=-1, keepdims=True)
        exp_scores = jnp.exp(scores - top_score)
        row_total = jnp.sum(exp_scores, axis=-1, keepdims=True)
        attn_probs = exp_scores / row_total
        head_out = dot(attn_probs.astype(bf16), value_head, 1, 0)
        return (head_out, (top_score + jnp.log(row_total))[:, 0])

    def head_backward(parts):
        query_head, key_head, value_head, grad_head, log_total = parts
        scores = head_scores(query_head, key_head)
        attn_probs = jnp.exp(scores - log_total[:, None])
        grad_value = dot(attn_probs.astype(bf16), grad_head, 0, 0)
        grad_probs = dot(grad_head, value_head, 1, 1)
        grad_scores = attn_probs * (
            grad_probs - jnp.sum(grad_probs * attn_probs, axis=-1, keepdims=True)
        )
        grad_low = grad_scores.astype(bf16)
        grad_query = dot(grad_low, key_head, 1, 0) * score_scale
        grad_key = dot(grad_low, query_head, 0, 0) * score_scale
        return (grad_query, grad_key, grad_value)

    head_outs, log_totals = lax.map(head_forward, (query_heads, key_heads, value_heads))
    attended = jnp.swapaxes(head_outs, 0, 1).reshape(length, D).astype(bf16)
    attended = dot(attended, dense_order, 1, 0).astype(bf16)
    stream_mid = stream + dot(attended, out_full, 1, 0)
    scale_two = lax.rsqrt(jnp.mean(stream_mid * stream_mid, axis=-1, keepdims=True) + epsilon)
    normed_two = stream_mid * scale_two
    expert_in = (normed_two * gain_two).astype(bf16)
    logits = dot(expert_in, router_full, 1, 1)
    chosen = jnp.stack([jnp.sum(p * logits, axis=-1) for p in pickers], axis=1)
    chosen_top = jnp.max(chosen, axis=1, keepdims=True)
    chosen_exp = jnp.exp(chosen - chosen_top)
    gate_values = chosen_exp / jnp.sum(chosen_exp, axis=1, keepdims=True)
    kept_float = jnp.stack(kept, axis=1)
    mix_weight = kept_float * gate_values

    arrived = send_rows(expert_in)
    slot_weight = sum(
        jnp.sum(places[j].astype(f32) * mix_weight[:, j : j + 1], axis=0) for j in range(2)
    ).reshape(experts, 1, capacity)
    slot_weight = jnp.concatenate(exchange([slot_weight[k] for k in range(experts)]), axis=0)
    chunk_ids = jnp.arange(dp_size, dtype=jnp.int32)
    if FF // dp_size == CHUNK:
        expert_down_in = expert_down_full.reshape(2, pairs, 1, group, CHUNK // 2, D)
        expert_a = lax.bitwise_xor(pair_of(chunk_ids), my_p)
        expert_b = lax.bitwise_xor(group_of(chunk_ids), my_g)
        expert_where = jnp.stack([jnp.zeros_like(my_c), my_c])
        shared_down_in = shared_down_full.reshape(2, 2, lanes, tall, CHUNK // expert_size, D)
        shared_a = lax.bitwise_xor(chunk_ids % 2, my_dp % 2)
        shared_b = lax.bitwise_xor(chunk_ids // 2, my_dp // 2)
        shared_where = jnp.stack([my_x, my_c])
    else:
        natural = (FF // CHUNK, 2, CHUNK // 2, D)
        expert_rows = order_of(expert_home, 2 * dp_size, FF)
        dense_rows = order_of(dense_home, devices, FF)
        expert_down_in = dot(expert_rows, expert_down_full.reshape(FF, D), 1, 0).astype(bf16)
        expert_down_in = expert_down_in.reshape(natural).swapaxes(0, 1)[:, None, None]
        shared_down_in = dot(dense_rows, shared_down_full.reshape(FF, D), 1, 0).astype(bf16)
        shared_down_in = shared_down_in.reshape(natural).swapaxes(0, 1)[:, None, None]
        chunk_ids = jnp.arange(FF // CHUNK, dtype=jnp.int32)
        expert_a = shared_a = jnp.zeros_like(chunk_ids)
        expert_b = shared_b = chunk_ids
        expert_where = shared_where = jnp.zeros((2,), jnp.int32)
    expert_blocks = 2 * dp_size if (D // (2 * dp_size)) % 16 == 0 else 2
    shared_blocks = 4 * lanes if (D // (4 * lanes)) % 16 == 0 else 2
    expert_out, grad_rows, grad_gates, expert_gu_grad, expert_down_grad = two_layers(
        expert_where,
        expert_a,
        expert_b,
        arrived,
        upstream_rows,
        slot_weight.reshape(experts * capacity, 1),
        expert_order,
        expert_gu_full,
        expert_down_in,
        expert_blocks,
        True,
    )
    shared_out, shared_dx, shared_gu_grad, shared_down_grad = two_layers(
        shared_where,
        shared_a,
        shared_b,
        expert_in,
        upstream,
        jnp.ones((length, 1), f32),
        dense_order,
        shared_gu_full,
        shared_down_in,
        shared_blocks,
        False,
    )

    def return_rows(values):
        values = values.reshape((experts, capacity) + values.shape[1:])
        return jnp.concatenate(exchange([values[k] for k in range(experts)]), axis=0)

    grad_gates = grad_gates.reshape(experts, 1, capacity)
    gate_back = jnp.concatenate(exchange([grad_gates[k] for k in range(experts)]), axis=0)
    buffer_rows = return_rows(grad_rows)
    returned = return_rows(expert_out)
    mixed = stream_mid + shared_out
    for j in range(2):
        mixed = mixed + mix_weight[:, j : j + 1] * dot(places[j], returned, 1, 0)
    mixed = mixed.astype(bf16)

    cotangent = upstream.astype(f32)
    gate_row = gate_back.reshape(1, experts * capacity)
    grad_gate = jnp.stack(
        [jnp.sum(places[j].astype(f32) * gate_row, axis=1) for j in range(2)], axis=1
    )
    grad_chosen = gate_values * (
        grad_gate - jnp.sum(gate_values * grad_gate, axis=1, keepdims=True)
    )
    grad_logits = sum(pickers[j] * grad_chosen[:, j : j + 1] for j in range(2)).astype(bf16)
    expert_in_ordered = dot(expert_in, dense_order, 1, 0).astype(bf16)
    router_grad = dot(expert_in_ordered, grad_logits, 0, 0)
    grad_expert_in = (
        shared_dx + dot(grad_logits, router_full, 1, 0) + dot(both_places, buffer_rows, 1, 0)
    )
    norm_second_grad = jnp.sum(grad_expert_in * normed_two, axis=0, keepdims=True)
    grad_mid = cotangent + norm_back(grad_expert_in * gain_two, normed_two, scale_two)
    grad_mid_low = grad_mid.astype(bf16)
    out_weight_grad = dot(attended, grad_mid_low, 0, 0)
    grad_attended = dot(grad_mid_low, out_full, 1, 1).astype(bf16)
    grad_attended = dot(grad_attended, dense_order, 1, 1).astype(bf16)
    grad_heads = jnp.swapaxes(grad_attended.reshape(length, HEADS, HEAD_DIM), 0, 1)
    grad_query, grad_key, grad_value = lax.map(
        head_backward, (query_heads, key_heads, value_heads, grad_heads, log_totals)
    )
    grad_query = rotate_back(jnp.swapaxes(grad_query, 0, 1), cosine_table, sine_table).reshape(
        length, D
    )
    grad_key = rotate_back(jnp.swapaxes(grad_key, 0, 1), cosine_table, sine_table).reshape(
        length, D
    )
    grad_value = jnp.swapaxes(grad_value, 0, 1).reshape(length, D)
    grad_projected = jnp.concatenate([grad_query, grad_key, grad_value], axis=-1).astype(bf16)
    qkv_grad = dot(normed_low, grad_projected, 0, 0)
    grad_normed = unpermute(dot(grad_projected, qkv_full[:, : 3 * D], 1, 1), dense_order)
    norm_first_grad = jnp.sum(grad_normed * normed_one, axis=0, keepdims=True)
    input_grad = grad_mid + norm_back(grad_normed * gain_one, normed_one, scale_one)

    def to_rows(row):
        high = row.astype(bf16)
        rest = (row - high.astype(f32)).astype(bf16)
        return dot(dense_order, high, 0, 1) + dot(dense_order, rest, 0, 1)

    def relative(grads):
        return grads.astype(bf16).reshape(2, 2 * lanes, tall, -1, grads.shape[-1])

    out_pack = jnp.concatenate(
        [
            out_weight_grad,
            jnp.pad(
                jnp.concatenate([to_rows(norm_second_grad), router_grad], axis=1),
                ((0, 0), (0, 127 - experts)),
            ),
        ],
        axis=1,
    )
    qkv_pack = jnp.concatenate(
        [qkv_grad, jnp.pad(to_rows(norm_first_grad), ((0, 0), (0, 127)))], axis=1
    )
    if expert_blocks == 2 * dp_size:
        expert_gu_grad = expert_gu_grad.reshape(2, pairs, group, 2, -1, FF)
    else:
        expert_gu_grad = expert_gu_grad.reshape(2, 2, pairs, group, -1, FF)
        expert_gu_grad = jnp.moveaxis(expert_gu_grad, 1, 3)
    shared_gu_grad = shared_gu_grad.reshape(
        (2, 2 * lanes, 2, tall, -1, FF)
        if shared_blocks == 4 * lanes
        else (2, 2, 2 * lanes, tall, -1, FF)
    )
    shared_gu_grad = jnp.moveaxis(shared_gu_grad, 2 if shared_blocks == 4 * lanes else 1, 3)
    if FF // dp_size == CHUNK:
        expert_down_grad = expert_down_grad.reshape(2, pairs, group, CHUNK // 2, D)
        shared_down_grad = shared_down_grad.reshape(2, 2 * lanes, tall, -1, D)
    else:
        expert_down_grad = expert_down_grad.reshape(2, -1, CHUNK // 2, D).swapaxes(0, 1)
        shared_down_grad = shared_down_grad.reshape(2, -1, CHUNK // 2, D).swapaxes(0, 1)
        expert_down_grad = dot(expert_rows, expert_down_grad.reshape(FF, D), 0, 0).astype(bf16)
        expert_down_grad = expert_down_grad.reshape(2, pairs, group, -1, D)
        shared_down_grad = dot(dense_rows, shared_down_grad.reshape(FF, D), 0, 0).astype(bf16)
        shared_down_grad = shared_down_grad.reshape(2, 2 * lanes, tall, -1, D)
    expert_gu_sum = scatter_expert(expert_gu_grad)
    expert_down_sum = scatter_expert(expert_down_grad)
    shared_gu_sum = scatter_dense(shared_gu_grad)
    shared_down_sum = scatter_dense(shared_down_grad)
    out_sum = scatter_dense(relative(out_pack))
    qkv_sum = scatter_dense(relative(qkv_pack))
    expert_gu_sum = jnp.moveaxis(expert_gu_sum, 2, 3).reshape(held, -1, 2 * FF).astype(f32)
    return (
        mixed,
        input_grad,
        qkv_sum[:, 3 * D],
        qkv_sum[:, : 3 * D],
        out_sum[:, :D],
        out_sum[:, D],
        out_sum[:, D + 1 : D + 1 + experts],
        jnp.moveaxis(shared_gu_sum, 0, 1).reshape(-1, 2 * FF),
        shared_down_sum,
        expert_gu_sum,
        expert_down_sum.reshape(held, -1, D).astype(f32),
    )


def solution(mesh):
    rows = P(AX, None)
    split = P("expert", "dp", None)
    in_specs = (rows,) * 4 + (P(AX), rows, rows, P(AX)) + (rows,) * 3 + (split,) * 2
    out_specs = (rows, rows, P(AX), rows, rows, P(AX)) + (rows,) * 3 + (split,) * 2
    inner = functools.partial(body, mesh.shape["dp"], mesh.shape["expert"])
    return jax.shard_map(inner, mesh=mesh, in_specs=in_specs, out_specs=out_specs, check_vma=False)
```

```python
import functools

import jax
import jax.numpy as jnp
from jax import lax
from jax.experimental import pallas as pl
from jax.experimental.pallas import tpu as pltpu
from jax.sharding import PartitionSpec as P

D = 768
HEADS = 12
HEAD_DIM = 64
FF = 2048
CHUNK = 256
PAIR = 2 * HEAD_DIM
SPAN = 256
BAND = 128
EXTRA = 16
AX = ("dp", "expert")
PAIR_LOW = True

epsilon = 1e-06
bf16 = jnp.bfloat16
f32 = jnp.float32


def dot(left, right, left_dim, right_dim, precision=None):
    return lax.dot_general(
        left,
        right,
        (((left_dim,), (right_dim,)), ((), ())),
        preferred_element_type=f32,
        precision=precision,
    )


def rope_tables(length):
    half_width = HEAD_DIM // 2
    frequency = 10000.0 ** (-jnp.arange(half_width, dtype=f32) / half_width)
    angles = jnp.arange(length, dtype=f32)[:, None] * frequency[None, :]
    return jnp.tile(jnp.cos(angles), (1, 4)), jnp.tile(jnp.sin(angles), (1, 4))


def swap_halves(values):
    first = lax.broadcasted_iota(jnp.int32, values.shape, 1) % HEAD_DIM < HEAD_DIM // 2
    up = pltpu.roll(values, PAIR - HEAD_DIM // 2, 1)
    down = pltpu.roll(values, HEAD_DIM // 2, 1)
    return up, down, first


def rotate(values, cosine, sine):
    up, down, first = swap_halves(values)
    return values * cosine + jnp.where(first, -up, down) * sine


def rotate_back(grads, cosine, sine):
    up, down, first = swap_halves(grads * sine)
    return grads * cosine + jnp.where(first, up, -down)


def norm_back(grad_normed, normed, scale):
    return scale * (grad_normed - normed * jnp.mean(grad_normed * normed, axis=-1, keepdims=True))


def unpermute(values, order):
    high = values.astype(bf16)
    rest = (values - high.astype(f32)).astype(bf16)
    return dot(high, order, 1, 1) + dot(rest, order, 1, 1)


def fill_bias(bias, column_ref, row_ref):
    length = bias.shape[0]
    query = lax.broadcasted_iota(jnp.int32, (length, length), 0)
    key = lax.broadcasted_iota(jnp.int32, (length, length), 1)
    allowed = (query >= key) & (column_ref[...] == row_ref[...])
    bias[...] = jnp.where(allowed, 0.0, -1000000000.0)


def bands(length):
    return [
        (slice(t, t + BAND), slice(max(0, t - SPAN), t + BAND)) for t in range(0, length, BAND)
    ]


def heads_of(values):
    lane = lax.broadcasted_iota(jnp.int32, values.shape, 1)
    zero = jnp.zeros_like(values)
    return jnp.where(lane < HEAD_DIM, values, zero), jnp.where(lane < HEAD_DIM, zero, values)


def attend_kernel(
    x_ref, wq_ref, wk_ref, wv_ref, cos_ref, sin_ref, column_ref, row_ref,
    q_ref, k_ref, v_ref, o_ref, lse_ref, bias,
):
    @pl.when(pl.program_id(0) == 0)
    def _():
        fill_bias(bias, column_ref, row_ref)

    x, cosine, sine = x_ref[...], cos_ref[...], sin_ref[...]
    query = rotate(dot(x, wq_ref[...], 1, 0), cosine, sine).astype(bf16)
    query = query * jnp.asarray(HEAD_DIM ** (-0.5), bf16)
    key = rotate(dot(x, wk_ref[...], 1, 0), cosine, sine).astype(bf16)
    value = dot(x, wv_ref[...], 1, 0).astype(bf16)
    q_ref[...], k_ref[...], v_ref[...] = query, key, value
    queries = heads_of(query)
    for rows, keys in bands(x.shape[0]):
        outs, totals = [], []
        for head in queries:
            scores = dot(head[rows], key[keys], 1, 1) + bias[rows, keys]
            top = jnp.max(scores, axis=-1, keepdims=True)
            weights = jnp.exp(scores - top)
            total = jnp.sum(weights, axis=-1, keepdims=True)
            probs = (weights * (1.0 / total)).astype(bf16)
            outs.append(dot(probs, value[keys], 1, 0))
            totals.append(jnp.broadcast_to(top + jnp.log(total), (BAND, PAIR)))
        lane = lax.broadcasted_iota(jnp.int32, (BAND, PAIR), 1)
        o_ref[rows, :] = jnp.where(lane < HEAD_DIM, outs[0], outs[1]).astype(bf16)
        lse_ref[rows, :] = jnp.where(lane < HEAD_DIM, totals[0], totals[1])


def attend(x, qkv, cosine, sine, column, row):
    length = x.shape[0]
    pairs = D // PAIR
    whole = lambda *shape: pl.BlockSpec(shape, lambda s: (0,) * len(shape))
    part = lambda n: pl.BlockSpec((D, PAIR), lambda s: (0, s + n * pairs))
    each = pl.BlockSpec((length, PAIR), lambda s: (0, s))
    return pl.pallas_call(
        attend_kernel,
        grid=(pairs,),
        in_specs=[
            whole(length, D), part(0), part(1), part(2), whole(length, PAIR),
            whole(length, PAIR), whole(length, 1), whole(1, length),
        ],
        out_specs=[each] * 5,
        out_shape=[jax.ShapeDtypeStruct((length, D), bf16)] * 4
        + [jax.ShapeDtypeStruct((length, D), f32)],
        scratch_shapes=[pltpu.VMEM((length, length), f32)],
        compiler_params=pltpu.CompilerParams(vmem_limit_bytes=40 << 20),
        cost_estimate=pl.CostEstimate(
            flops=20_000_000_000, bytes_accessed=10 * D * length + 6 * D * D, transcendentals=0
        ),
        name="attend",
    )(x, qkv, qkv, qkv, cosine, sine, column, row)


def attend_back_kernel(
    q_ref, k_ref, v_ref, lse_ref, grad_ref, x_ref, wq_ref, wk_ref, wv_ref, cos_ref, sin_ref,
    column_ref, row_ref, order_ref, tokens_ref, gain_ref, mid_ref,
    dw0_ref, dw1_ref, dx_ref, dgain_ref, bias, dq, dk, dv, normed_sum,
):
    step = pl.program_id(0)
    dw_refs = (dw0_ref, dw1_ref)

    @pl.when(step == 0)
    def _():
        fill_bias(bias, column_ref, row_ref)
        normed_sum[...] = jnp.zeros_like(normed_sum)

    key, value = k_ref[...], v_ref[...]
    queries, keys_of, grads = heads_of(q_ref[...]), heads_of(key), heads_of(grad_ref[...])
    dk[...] = jnp.zeros_like(dk)
    dv[...] = jnp.zeros_like(dv)
    for rows, keys in bands(key.shape[0]):
        query_sum = key_sum = value_sum = 0.0
        for n in range(2):
            head, grad = queries[n][rows], grads[n][rows]
            scores = dot(head, key[keys], 1, 1) + bias[rows, keys]
            probs = jnp.exp(scores - lse_ref[rows, n * HEAD_DIM : n * HEAD_DIM + 1])
            grad_probs = dot(grad, value[keys], 1, 1)
            shift = jnp.sum(grad_probs * probs, axis=-1, keepdims=True)
            low = (probs * (grad_probs - shift)).astype(bf16)
            value_sum += dot(probs.astype(bf16), grad, 0, 0)
            query_sum += dot(low, keys_of[n][keys], 1, 0)
            key_sum += dot(low, head, 0, 0)
        dq[rows, :] = query_sum * HEAD_DIM ** (-0.5)
        dk[keys, :] += key_sum
        dv[keys, :] += value_sum
    cosine, sine = cos_ref[...], sin_ref[...]
    parts = [
        rotate_back(dq[...], cosine, sine).astype(bf16),
        rotate_back(dk[...], cosine, sine).astype(bf16),
        dv[...].astype(bf16),
    ]
    x = x_ref[...]
    blocks, _, per, _ = dw_refs[0].shape
    for n, (part, weight_ref) in enumerate(zip(parts, (wq_ref, wk_ref, wv_ref), strict=True)):
        normed_sum[...] += dot(part, weight_ref[...], 1, 1)
        weight_grad = dot(x, part, 0, 0).astype(bf16)
        for i in range(2):
            for k in range(blocks):
                place = (i * blocks + k) * per
                dw_refs[i][k, n] = weight_grad[place : place + per]

    @pl.when(step == pl.num_programs(0) - 1)
    def _():
        stream = tokens_ref[...].astype(f32)
        scale = lax.rsqrt(jnp.mean(stream * stream, axis=-1, keepdims=True) + epsilon)
        normed = stream * scale
        grad_normed = unpermute(normed_sum[...], order_ref[...])
        dgain_ref[...] = jnp.sum(grad_normed * normed, axis=0, keepdims=True)
        dx_ref[...] = mid_ref[...] + norm_back(grad_normed * gain_ref[...], normed, scale)


def attend_back(
    query, key, value, lse, grad, x, qkv, cosine, sine, column, row, order, tokens, gain, mid, blocks
):
    length = x.shape[0]
    pairs = D // PAIR
    whole = lambda *shape: pl.BlockSpec(shape, lambda s: (0,) * len(shape))
    part = lambda n: pl.BlockSpec((D, PAIR), lambda s: (0, s + n * pairs))
    each = pl.BlockSpec((length, PAIR), lambda s: (0, s))
    return pl.pallas_call(
        attend_back_kernel,
        grid=(pairs,),
        in_specs=[
            each, each, each, each, each, whole(length, D), part(0), part(1), part(2),
            whole(length, PAIR), whole(length, PAIR), whole(length, 1), whole(1, length),
            whole(D, D), whole(length, D), whole(1, D), whole(length, D),
        ],
        out_specs=[
            pl.BlockSpec((blocks, 3, D // 2 // blocks, PAIR), lambda s: (0, 0, 0, s)),
            pl.BlockSpec((blocks, 3, D // 2 // blocks, PAIR), lambda s: (0, 0, 0, s)),
            whole(length, D),
            whole(1, D),
        ],
        out_shape=[
            jax.ShapeDtypeStruct((blocks, 3, D // 2 // blocks, D), bf16),
            jax.ShapeDtypeStruct((blocks, 3, D // 2 // blocks, D), bf16),
            jax.ShapeDtypeStruct((length, D), f32),
            jax.ShapeDtypeStruct((1, D), f32),
        ],
        scratch_shapes=[pltpu.VMEM((length, length), f32)]
        + [pltpu.VMEM((length, PAIR), f32)] * 3
        + [pltpu.VMEM((length, D), f32)],
        compiler_params=pltpu.CompilerParams(vmem_limit_bytes=48 << 20),
        cost_estimate=pl.CostEstimate(
            flops=40_000_000_000, bytes_accessed=20 * D * length + 12 * D * D, transcendentals=0
        ),
        name="attend_back",
    )(
        query, key, value, lse, grad, x, qkv, qkv, qkv, cosine, sine, column, row, order, tokens,
        gain, mid,
    )


def split_three(values, exact=False):
    parts = []
    for _ in range(3):
        high = lax.reduce_precision(values, 8, 7) if exact else values.astype(bf16).astype(f32)
        parts.append(high.astype(bf16))
        values = values - high
    return parts


def branch(x, u, gate_weight, up_weight, down):
    gate = dot(x, gate_weight, 1, 0)
    up = dot(x, up_weight, 1, 0)
    sigmoid = jax.nn.sigmoid(gate)
    act = gate * sigmoid
    slope = sigmoid * (1.0 + gate * (1.0 - sigmoid))
    grad_hidden = dot(u, down, 1, 1)
    hidden = (act * up).astype(bf16)
    return hidden, (grad_hidden * up * slope).astype(bf16), (grad_hidden * act).astype(bf16)


def accumulate(total, part):
    step = pl.program_id(0)

    @pl.when(step == 0)
    def _():
        total[...] = part

    @pl.when(step > 0)
    def _():
        total[...] += part


def shared_kernel(
    where_ref, a_ref, b_ref, x_ref, u_ref, order_ref, gate_ref, up_ref, *refs, cores, lanes
):
    down_refs, (out_ref, dx_ref), refs = refs[:cores], refs[cores : cores + 2], refs[cores + 2 :]
    dgu_refs, dd_refs, xp = refs[:cores], refs[cores : 2 * cores], refs[2 * cores]

    @pl.when(pl.program_id(0) == 0)
    def _():
        xp[...] = dot(x_ref[...], order_ref[...], 1, 0).astype(bf16)

    swap = where_ref[1] == 1
    slots = [lax.bitwise_xor(n, where_ref[0]) for n in range(lanes)]
    pieces = []
    for n in range(lanes):
        found = [r[0, slots[n], 0] for r in down_refs]
        if cores == 2:
            found = [jnp.where(swap, found[1], found[0]), jnp.where(swap, found[0], found[1])]
        pieces.extend(found)
    down = jnp.concatenate(pieces, axis=0)
    x, u = x_ref[...], u_ref[...]
    hidden, grad_gate, grad_up = branch(x, u, gate_ref[...], up_ref[...], down)
    accumulate(out_ref, dot(hidden, down, 1, 0))
    accumulate(dx_ref, dot(grad_gate, gate_ref[...], 1, 1) + dot(grad_up, up_ref[...], 1, 1))
    grad_down = dot(hidden, u, 0, 0).astype(bf16)
    per = grad_down.shape[0] // (cores * lanes)
    for n in range(lanes):
        found = [grad_down[(n * cores + i) * per : (n * cores + i + 1) * per] for i in range(cores)]
        if cores == 2:
            found = [jnp.where(swap, found[1], found[0]), jnp.where(swap, found[0], found[1])]
        for i in range(cores):
            dd_refs[i][0, slots[n], 0] = found[i]
    x = xp[...]
    blocks, _, per, _ = dgu_refs[0].shape
    for half, grads in ((0, grad_gate), (1, grad_up)):
        weight_grad = dot(x, grads, 0, 0).astype(bf16)
        for i in range(cores):
            for k in range(blocks):
                place = (i * blocks + k) * per
                dgu_refs[i][k, half] = weight_grad[place : place + per]


def whole(*shape):
    return pl.BlockSpec(shape, lambda *_: (0,) * len(shape))


def shared_branch(where, a_index, b_index, x, u, order, gate_up, downs, blocks):
    rows = x.shape[0]
    cores = len(downs)
    a_size, lanes, b_size, per_down, _ = downs[0].shape
    chunks = a_size * b_size
    width = FF // chunks
    per = D // cores // blocks
    down_spec = pl.BlockSpec((1, lanes, 1, per_down, D), lambda s, q, a, b: (a[s], 0, b[s], 0, 0))
    return pl.pallas_call(
        functools.partial(shared_kernel, cores=cores, lanes=lanes),
        grid_spec=pltpu.PrefetchScalarGridSpec(
            num_scalar_prefetch=3,
            grid=(chunks,),
            in_specs=[
                whole(rows, D),
                whole(rows, D),
                whole(D, D),
                pl.BlockSpec((D, width), lambda s, *_: (0, s)),
                pl.BlockSpec((D, width), lambda s, *_: (0, s + chunks)),
            ]
            + [down_spec] * cores,
            out_specs=[whole(rows, D)] * 2
            + [pl.BlockSpec((blocks, 2, per, width), lambda s, *_: (0, 0, 0, s))] * cores
            + [down_spec] * cores,
            scratch_shapes=[pltpu.VMEM((rows, D), bf16)],
        ),
        out_shape=[jax.ShapeDtypeStruct((rows, D), f32)] * 2
        + [jax.ShapeDtypeStruct((blocks, 2, per, FF), bf16)] * cores
        + [jax.ShapeDtypeStruct(downs[0].shape, bf16)] * cores,
        compiler_params=pltpu.CompilerParams(vmem_limit_bytes=48 << 20),
        cost_estimate=pl.CostEstimate(
            flops=2 * 9 * rows * D * FF, bytes_accessed=12 * D * FF, transcendentals=rows * FF
        ),
        name="shared_branch",
    )(where, a_index, b_index, x, u, order, gate_up, gate_up, *downs)


def expert_kernel(core_ref, columns_ref, x_ref, u_ref, w_ref, order_ref, *refs, cores, pairs, blocks):
    parts = cores * pairs
    gate_refs, up_refs, down_refs = (refs[i * parts : (i + 1) * parts] for i in range(3))
    out_ref, dx_ref = refs[3 * parts : 3 * parts + 2]
    refs = refs[3 * parts + 2 :]
    dgu_refs, dd_refs = refs[:parts], refs[parts : 2 * parts]
    xp, go, out_sum, dx_sum = refs[2 * parts :]
    step = pl.program_id(0)
    per_pair = pl.num_programs(0) // pairs

    owners, capacity = x_ref.shape[0], x_ref.shape[1] - EXTRA

    @pl.when(step == 0)
    def _():
        arrived = x_ref[:, :capacity, :].reshape(owners * capacity, D)
        xp[...] = dot(arrived, order_ref[...], 1, 0).astype(bf16)
        go[...] = (u_ref[...].astype(f32) * w_ref[...]).astype(bf16)

    def pick(values):
        chosen = values[0]
        for m in range(1, pairs):
            chosen = jnp.where(step >= m * per_pair, values[m], chosen)
        return chosen

    x, grad_out = xp[...], go[...]
    gate_weight = jnp.concatenate([r[...] for r in gate_refs], axis=0)
    up_weight = jnp.concatenate([r[...] for r in up_refs], axis=0)
    downs = [pick([down_refs[i * pairs + m][0] for m in range(pairs)]) for i in range(cores)]
    swap = core_ref[0] == 1
    if cores == 2:
        downs = [jnp.where(swap, downs[1], downs[0]), jnp.where(swap, downs[0], downs[1])]
    down = jnp.concatenate(downs, axis=0)
    hidden, grad_gate, grad_up = branch(x, grad_out, gate_weight, up_weight, down)
    accumulate(out_sum, dot(hidden, down, 1, 0))
    accumulate(dx_sum, dot(grad_gate, gate_weight, 1, 1) + dot(grad_up, up_weight, 1, 1))
    grad_down = dot(hidden, grad_out, 0, 0).astype(bf16)
    if cores == 2:
        half = grad_down.shape[0] // 2
        low, high = grad_down[:half], grad_down[half:]
        grad_downs = [jnp.where(swap, high, low), jnp.where(swap, low, high)]
    else:
        grad_downs = [grad_down]
    for m in range(pairs):

        @pl.when((step >= m * per_pair) & (step < (m + 1) * per_pair))
        def _(m=m):
            for i in range(cores):
                dd_refs[i * pairs + m][0] = grad_downs[i]

    for half, grads in ((0, grad_gate), (1, grad_up)):
        weight_grad = dot(x, grads, 0, 0).astype(bf16)
        per = D // parts // blocks
        for n in range(parts):
            for k in range(blocks):
                place = (n * blocks + k) * per
                dgu_refs[n][k, half] = weight_grad[place : place + per]

    @pl.when(step == pl.num_programs(0) - 1)
    def _():
        out_low = out_sum[...].astype(bf16)
        out_ref[...] = out_low
        grad_rows = dot(dx_sum[...].astype(bf16), order_ref[...], 1, 1).astype(bf16)
        product = u_ref[...].astype(f32) * out_low.astype(f32)
        grad_gates = dot(jnp.ones((8, D), f32), product, 1, 1, lax.Precision.HIGHEST)
        parts = split_three(grad_gates[0:1])
        blank = jnp.zeros((EXTRA - 3, capacity), bf16)
        for e in range(owners):
            dx_ref[e, :capacity] = grad_rows[e * capacity : (e + 1) * capacity]
            lanes = slice(e * capacity, (e + 1) * capacity)
            dx_ref[e, capacity:, :capacity] = jnp.concatenate([p[:, lanes] for p in parts] + [blank], axis=0)
            dx_ref[e, capacity:, capacity:] = jnp.zeros((EXTRA, D - capacity), bf16)


def expert_branch(core, columns, x, u, w, order, gate_ups, downs, cores, blocks):
    rows = u.shape[0]
    parts = len(gate_ups)
    pairs = parts // cores
    chunks = columns.shape[0]
    width = FF // chunks
    per_pair = chunks // pairs
    part_rows = D // parts
    per_down = width // cores

    def down_spec(m):
        place = lambda s, *_: (jnp.clip(s - m * per_pair, 0, per_pair - 1), 0, 0)
        return pl.BlockSpec((1, per_down, D), place)

    down_specs = [down_spec(n % pairs) for n in range(parts)]
    return pl.pallas_call(
        functools.partial(expert_kernel, cores=cores, pairs=pairs, blocks=blocks),
        grid_spec=pltpu.PrefetchScalarGridSpec(
            num_scalar_prefetch=2,
            grid=(chunks,),
            in_specs=[whole(*x.shape), whole(rows, D), whole(rows, 1), whole(D, D)]
            + [pl.BlockSpec((part_rows, width), lambda s, c, q: (0, q[s]))] * parts
            + [pl.BlockSpec((part_rows, width), lambda s, c, q: (0, q[s] + chunks))] * parts
            + down_specs,
            out_specs=[whole(rows, D), whole(*x.shape)]
            + [
                pl.BlockSpec(
                    (blocks, 2, part_rows // blocks, width), lambda s, c, q: (0, 0, 0, q[s])
                )
            ]
            * parts
            + down_specs,
            scratch_shapes=[
                pltpu.VMEM((rows, D), bf16),
                pltpu.VMEM((rows, D), bf16),
                pltpu.VMEM((rows, D), f32),
                pltpu.VMEM((rows, D), f32),
            ],
        ),
        out_shape=[
            jax.ShapeDtypeStruct((rows, D), bf16),
            jax.ShapeDtypeStruct(x.shape, bf16),
        ]
        + [jax.ShapeDtypeStruct((blocks, 2, part_rows // blocks, FF), bf16)] * parts
        + [jax.ShapeDtypeStruct((per_pair, per_down, D), bf16)] * parts,
        compiler_params=pltpu.CompilerParams(vmem_limit_bytes=56 << 20),
        cost_estimate=pl.CostEstimate(
            flops=2 * 9 * rows * D * FF,
            bytes_accessed=12 * D * FF + 12 * rows * D,
            transcendentals=rows * FF,
        ),
        name="expert_branch",
    )(core, columns, x, u, w, order, *gate_ups, *gate_ups, *downs)


def body(
    dp_size,
    expert_size,
    tokens,
    segment_ids,
    expert_ids,
    upstream,
    norm_first,
    qkv_weight,
    out_weight,
    norm_second,
    router_weight,
    shared_gate_up,
    shared_down,
    expert_gate_up,
    expert_down,
):
    devices = dp_size * expert_size
    lanes = expert_size // 2
    length = tokens.shape[0]
    experts = expert_gate_up.shape[0] * expert_size
    held = expert_gate_up.shape[0]
    group = experts // lanes
    pairs = dp_size // group
    capacity = length * 2 // experts
    tall = dp_size // 2

    me = lax.axis_index(AX).astype(jnp.int32)
    my_dp, my_expert = me // expert_size, me % expert_size
    my_x, my_c = my_expert // 2, my_expert % 2
    if PAIR_LOW:
        pair_of, group_of = (lambda d: d % pairs), (lambda d: d // pairs)
        dp_of = lambda p, g: g * pairs + p
    else:
        pair_of, group_of = (lambda d: d // group), (lambda d: d % group)
        dp_of = lambda p, g: p * group + g
    my_p, my_g = pair_of(my_dp), group_of(my_dp)

    def hop(values, offset):
        return lax.ppermute(values, AX, [(s, s ^ offset) for s in range(devices)])

    def arrive(values, offsets, after):
        blocks = [hop(v, o) for v, o in zip(values, offsets, strict=True)]
        if after:
            blocks = lax.optimization_barrier((blocks,) + after)[0]
        return blocks

    def spread(values, offsets, after=()):
        others = offsets[1:]
        return jnp.stack([values] + arrive([values] * len(others), others, after))

    def collect(blocks, offsets, after=()):
        others = offsets[1:]
        total = blocks[0].astype(f32)
        for block in arrive([blocks[i + 1] for i in range(len(others))], others, after):
            total = total + block.astype(f32)
        return total

    tall_offsets = [2 * i * expert_size for i in range(tall)]
    flat_offsets = [y * expert_size + 2 * x for y in range(2) for x in range(lanes)]
    pair_offsets = [dp_of(p, 0) * expert_size for p in range(pairs)]
    group_offsets = [dp_of(0, g) * expert_size for g in range(group)]

    def gate(values, *earlier):
        return lax.optimization_barrier((values,) + earlier)[0]

    def dense_home(position):
        i, j, c = position % tall, position // tall % (2 * lanes), position // tall // (2 * lanes)
        offset = (2 * i + j // lanes) * expert_size + 2 * (j % lanes) + c
        return lax.bitwise_xor(me, offset)

    def gather_expert(shard):
        halves = shard.reshape(held, 2, shard.shape[1] // 2, shard.shape[2])
        mine = lax.dynamic_index_in_dim(halves, my_c, 1, keepdims=False)
        other = hop(lax.dynamic_index_in_dim(halves, 1 - my_c, 1, keepdims=False), 1)
        all_held = jnp.concatenate(
            [jnp.where(my_c == 0, mine, other), jnp.where(my_c == 0, other, mine)], axis=0
        )
        parts = [
            lax.dynamic_index_in_dim(all_held, lax.bitwise_xor(my_g, g), 0, keepdims=False)
            for g in range(group)
        ]
        return parts

    def swap_groups(parts, after=()):
        blocks = arrive([parts[g] for g in range(1, group)], group_offsets[1:], after)
        return jnp.stack([parts[0]] + blocks)

    def settle_expert(parts):
        keep = [
            lax.dynamic_index_in_dim(parts, lax.bitwise_xor(my_g, my_c * held + j), 0)
            for j in range(held)
        ]
        give = [
            lax.dynamic_index_in_dim(parts, lax.bitwise_xor(my_g, (1 - my_c) * held + j), 0)
            for j in range(held)
        ]
        keep = jnp.concatenate(keep, axis=0)
        take = hop(jnp.concatenate(give, axis=0), 1)
        return jnp.stack([jnp.where(my_c == 0, keep, take), jnp.where(my_c == 0, take, keep)], axis=1)

    def expert_home(position):
        g, p, c = position % group, position // group % pairs, position // group // pairs
        dp = dp_of(lax.bitwise_xor(my_p, p), lax.bitwise_xor(my_g, g))
        return dp * 2 + lax.bitwise_xor(my_c, c)

    def order_of(home, blocks, width=D):
        per = width // blocks
        column = jnp.arange(width, dtype=jnp.int32)
        source = home(column // per) * per + column % per
        return (jnp.arange(width, dtype=jnp.int32)[:, None] == source[None, :]).astype(bf16)

    owners = [
        [dp_of(p, e % group) * expert_size + 2 * (e // group) + c for e in range(experts)]
        for p in range(pairs)
        for c in range(2)
    ]

    def exchange(rows):
        rows = rows.reshape((experts, -1, D))
        return lax.all_to_all(rows, AX, 0, 0, axis_index_groups=owners, tiled=True)

    dense_order = order_of(dense_home, devices)
    expert_order = order_of(expert_home, 2 * dp_size)

    def by_flat(grads):
        _, parts, _, width = grads.shape
        return jnp.swapaxes(grads.reshape(parts, 2 * lanes, -1, width), 0, 1)

    def by_tall(grads):
        parts, _, width = grads.shape
        return jnp.swapaxes(grads.reshape(parts, tall, -1, width), 0, 1)

    small = jnp.concatenate(
        [norm_first[:, None], norm_second[:, None], router_weight], axis=1
    )
    small = jnp.pad(small, ((0, 0), (0, 128 - small.shape[1])))
    qkv_full = spread(jnp.concatenate([qkv_weight, small, out_weight], axis=1), tall_offsets)
    gu_parts, down_parts = gather_expert(expert_gate_up), gather_expert(expert_down)
    qkv_full = spread(gate(qkv_full, gu_parts, down_parts), flat_offsets)
    expert_gu, expert_down = swap_groups(gu_parts), swap_groups(down_parts)
    shared_gu_full = lax.all_gather(shared_gate_up, AX, axis=0, tiled=True)
    shared_down_full = spread(gate(shared_down, gu_parts), tall_offsets)

    columns = jnp.arange(experts, dtype=jnp.int32)
    pickers = [(expert_ids[:, j : j + 1] == columns[None, :]).astype(f32) for j in range(2)]
    position = jnp.arange(length)
    earlier = (position[:, None] > position[None, :]).astype(bf16)
    counts = dot(earlier, (pickers[0] + pickers[1]).astype(bf16), 1, 0)
    kept, places = [], []
    for j in range(2):
        rank = jnp.sum(counts * pickers[j], axis=1).astype(jnp.int32)
        ids = expert_ids[:, j]
        kept_mask = rank < capacity
        slot = jnp.where(kept_mask, ids * capacity + rank, -1)
        kept.append(kept_mask.astype(f32))
        places.append(
            (slot[:, None] == jnp.arange(experts * capacity, dtype=jnp.int32)[None, :]).astype(bf16)
        )
    both_places = places[0] + places[1]

    def to_slots(values):
        return dot(both_places, values, 0, 0).astype(bf16)

    upstream_slots = to_slots(upstream)
    qkv_full = spread(gate(qkv_full, expert_gu, expert_down), [0, 1]).reshape(D, 4 * D + 128)
    out_full = qkv_full[:, 3 * D + 128 :]
    upstream_rows = exchange(gate(upstream_slots, qkv_full)).reshape(-1, D)

    small_full = dot(qkv_full[:, 3 * D : 3 * D + 128], dense_order, 0, 1)
    gain_one, gain_two = small_full[0:1], small_full[1:2]
    router_full = small_full[2 : 2 + experts].astype(bf16)
    stream = tokens.astype(f32)
    scale_one = lax.rsqrt(jnp.mean(stream * stream, axis=-1, keepdims=True) + epsilon)
    normed_one = stream * scale_one
    normed_low = (normed_one * gain_one).astype(bf16)
    normed_low = dot(normed_low, dense_order, 1, 0).astype(bf16)
    cosine, sine = rope_tables(length)
    column, row = segment_ids.reshape(length, 1), segment_ids
    ready = gate(normed_low, upstream_slots)
    query, key, value, attended, lse = attend(ready, qkv_full, cosine, sine, column, row)
    shared_down_full = spread(gate(shared_down_full, qkv_full), flat_offsets, (attended,))
    down_pairs = [expert_down] + arrive([expert_down] * (pairs - 1), pair_offsets[1:], (attended,))
    attended = gate(attended, upstream_rows, down_pairs, shared_down_full)
    attended = dot(attended, dense_order, 1, 0).astype(bf16)
    stream_mid = stream + dot(attended, out_full, 1, 0)
    scale_two = lax.rsqrt(jnp.mean(stream_mid * stream_mid, axis=-1, keepdims=True) + epsilon)
    normed_two = stream_mid * scale_two
    expert_in = (normed_two * gain_two).astype(bf16)
    logits = dot(expert_in, router_full, 1, 1)
    chosen = jnp.stack([jnp.sum(p * logits, axis=-1) for p in pickers], axis=1)
    chosen_top = jnp.max(chosen, axis=1, keepdims=True)
    chosen_exp = jnp.exp(chosen - chosen_top)
    gate_values = chosen_exp / jnp.sum(chosen_exp, axis=1, keepdims=True)
    kept_float = jnp.stack(kept, axis=1)
    mix_weight = kept_float * gate_values

    in_slots = to_slots(expert_in)
    slot_weight = sum(
        jnp.sum(places[j].astype(f32) * mix_weight[:, j : j + 1], axis=0) for j in range(2)
    )
    slot_weight = jnp.stack(split_three(slot_weight.reshape(experts, capacity), True), axis=1)
    slot_weight = jnp.pad(slot_weight, ((0, 0), (0, EXTRA - 3), (0, D - capacity)))
    in_slots = jnp.concatenate([in_slots.reshape(experts, capacity, D), slot_weight], axis=1)
    arrived = exchange(in_slots)
    slot_weight = jnp.sum(arrived[:, capacity : capacity + 3, :capacity].astype(f32), axis=1)
    slot_weight = slot_weight.reshape(experts * capacity, 1)
    relative = FF // dp_size == CHUNK
    dense_blocks = 2 * lanes if (D // (4 * lanes)) % 16 == 0 else 1
    shared_downs = [shared_down_full, hop(shared_down_full, 1)]
    if relative:
        shared_downs = [v.reshape(2, lanes, tall, -1, D) for v in shared_downs]
        place = jnp.arange(dp_size, dtype=jnp.int32)
        shared_a = lax.bitwise_xor(place % 2, my_dp % 2)
        shared_b = lax.bitwise_xor(place // 2, my_dp // 2)
        shared_where = jnp.stack([my_x, my_c])
    else:
        dense_rows = order_of(dense_home, devices, FF)
        shared_downs = jnp.stack(shared_downs).reshape(FF, D)
        shared_downs = dot(dense_rows, shared_downs, 1, 0).astype(bf16)
        shared_downs = [shared_downs.reshape(1, 1, -1, CHUNK, D)]
        shared_b = jnp.arange(FF // CHUNK, dtype=jnp.int32)
        shared_a = jnp.zeros_like(shared_b)
        shared_where = jnp.zeros((2,), jnp.int32)
    results = shared_branch(
        shared_where, shared_a, shared_b, gate(expert_in, in_slots), upstream, dense_order,
        shared_gu_full, shared_downs, dense_blocks if relative else 1,
    )
    shared_out, shared_dx = results[:2]
    if relative:
        shared_gu_grad, shared_down_grad = results[2:4], results[4:]
        if dense_blocks == 1:
            shared_gu_grad = [by_flat(g) for g in shared_gu_grad]
        shared_down_grad = [g.reshape(2 * lanes, -1, D) for g in shared_down_grad]
    else:
        shared_gu_grad = [by_flat(results[2][:, :, i * (D // 2) : (i + 1) * (D // 2)]) for i in range(2)]
        shared_down_grad = dot(dense_rows, results[3].reshape(FF, D), 0, 0).astype(bf16)
        shared_down_grad = list(shared_down_grad.reshape(2, 2 * lanes, -1, D))
    shared_gu_sum = collect(shared_gu_grad, [0, 1]).astype(bf16)
    shared_down_sum = collect(shared_down_grad, [0, 1]).astype(bf16)
    sent = (shared_gu_sum, shared_down_sum)
    upstream_rows = gate(upstream_rows, sent)

    gu_pairs = [expert_gu] + arrive(
        [gate(expert_gu, down_pairs)] * (pairs - 1), pair_offsets[1:], sent
    )
    gu_in = gu_pairs + [hop(v, 1) for v in gu_pairs]
    down_in = down_pairs + [hop(v, 1) for v in down_pairs]
    shards = 2 * pairs
    if relative:
        gu_in = [v.reshape(-1, 2 * FF) for v in gu_in]
        cores, blocks = 2, group
        place = jnp.arange(dp_size, dtype=jnp.int32)
        chunk_columns = dp_of(
            lax.bitwise_xor(place // group, my_p), lax.bitwise_xor(place % group, my_g)
        )
    else:
        expert_rows = order_of(expert_home, 2 * dp_size, FF)
        gu_in = [jnp.concatenate(gu_in, axis=0).reshape(D, 2 * FF)]
        down_in = jnp.concatenate(down_in, axis=0).reshape(FF, D)
        down_in = [dot(expert_rows, down_in, 1, 0).astype(bf16).reshape(-1, CHUNK, D)]
        cores, blocks = 1, 1
        chunk_columns = jnp.arange(FF // CHUNK, dtype=jnp.int32)
    results = expert_branch(
        my_c.reshape(1), chunk_columns, arrived, upstream_rows, slot_weight, expert_order, gu_in,
        down_in, cores, blocks,
    )
    expert_out, grad_rows = results[:2]
    gu_grads, down_grads = results[2 : 2 + len(gu_in)], results[2 + len(gu_in) :]
    if not relative:
        gu_grads = gu_grads[0].reshape(2, shards, group, -1, FF)
        gu_grads = [jnp.swapaxes(gu_grads[:, n], 0, 1) for n in range(shards)]
        down_grads = dot(expert_rows, down_grads[0].reshape(FF, D), 0, 0).astype(bf16)
        down_grads = [down_grads.reshape(shards, group, -1, D)[n] for n in range(shards)]

    shared_gu_sum = collect(shared_gu_sum, flat_offsets, (expert_out,)).astype(bf16)
    shared_down_sum = collect(shared_down_sum, flat_offsets, (expert_out,)).astype(bf16)
    buffer_rows = exchange(grad_rows)
    returned = exchange(gate(expert_out, buffer_rows)).reshape(-1, D)
    gu_sums = [collect(gu_grads[m::pairs], [0, 1]).astype(bf16) for m in range(pairs)]
    down_sums = [collect(down_grads[m::pairs], [0, 1]).astype(bf16) for m in range(pairs)]
    buffer_rows = gate(buffer_rows, gu_sums, down_sums, shared_gu_sum, shared_down_sum)
    gate_row = jnp.sum(buffer_rows[:, capacity : capacity + 3, :capacity].astype(f32), axis=1)
    buffer_rows = buffer_rows[:, :capacity].reshape(-1, D)

    cotangent = upstream.astype(f32)
    gate_row = gate_row.reshape(1, experts * capacity)
    grad_gate = jnp.stack(
        [jnp.sum(places[j].astype(f32) * gate_row, axis=1) for j in range(2)], axis=1
    )
    grad_chosen = gate_values * (
        grad_gate - jnp.sum(gate_values * grad_gate, axis=1, keepdims=True)
    )
    grad_logits = sum(pickers[j] * grad_chosen[:, j : j + 1] for j in range(2)).astype(bf16)
    router_grad = dot(grad_logits, expert_in, 0, 0)
    grad_expert_in = (
        shared_dx + dot(grad_logits, router_full, 1, 0) + dot(both_places, buffer_rows, 1, 0)
    )
    norm_second_grad = jnp.sum(grad_expert_in * normed_two, axis=0, keepdims=True)
    grad_mid = cotangent + norm_back(grad_expert_in * gain_two, normed_two, scale_two)
    grad_mid_low = grad_mid.astype(bf16)
    out_weight_grad = dot(attended, grad_mid_low, 0, 0)
    grad_attended = dot(grad_mid_low, out_full, 1, 1).astype(bf16)
    grad_attended = dot(grad_attended, dense_order, 1, 1).astype(bf16)
    out_weight_grad = out_weight_grad.astype(bf16).reshape(2, 2 * lanes, tall, -1, D)
    *qkv_grad, input_grad, norm_first_grad = attend_back(
        gate(query, out_weight_grad), key, value, lse, grad_attended, normed_low, qkv_full, cosine, sine, column, row,
        dense_order, tokens, gain_one, grad_mid, dense_blocks,
    )

    small_grad = jnp.concatenate([norm_first_grad, norm_second_grad, router_grad], axis=0)
    small_grad = jnp.swapaxes(small_grad.reshape(experts + 2, devices, D // devices), 0, 1)
    small_grad = gate(small_grad.reshape(devices, -1), returned)
    small_sum = jnp.sum(lax.all_to_all(small_grad, AX, 0, 0, tiled=True), axis=0)
    small_sum = small_sum.reshape(experts + 2, D // devices)

    if dense_blocks == 1:
        qkv_grad = [by_flat(g) for g in qkv_grad]
    done = (input_grad,)
    qkv_sum = collect(gate(qkv_grad, returned), [0, 1]).astype(bf16)
    out_sum = collect(out_weight_grad, [0, 1], done).astype(bf16)
    qkv_sum = collect(qkv_sum, flat_offsets).astype(bf16)
    out_sum = collect(out_sum, flat_offsets).astype(bf16)
    shared_gu_sum = collect(by_tall(shared_gu_sum), tall_offsets, done)
    shared_down_sum = collect(shared_down_sum.reshape(tall, -1, D), tall_offsets, done)
    mixed = stream_mid + shared_out
    for j in range(2):
        mixed = mixed + mix_weight[:, j : j + 1] * dot(places[j], returned, 1, 0)
    mixed = mixed.astype(bf16)
    expert_gu_sum = collect(gu_sums, pair_offsets, done).astype(bf16)
    expert_down_sum = collect(down_sums, pair_offsets, done).astype(bf16)
    expert_gu_sum = settle_expert(swap_groups(expert_gu_sum))
    expert_down_sum = settle_expert(swap_groups(expert_down_sum))
    out_sum = collect(out_sum, tall_offsets)
    qkv_sum = collect(gate(by_tall(qkv_sum), small_sum), tall_offsets)
    expert_gu_sum = jnp.moveaxis(expert_gu_sum, 2, 3).reshape(held, -1, 2 * FF).astype(f32)
    return (
        mixed,
        input_grad,
        small_sum[0],
        jnp.moveaxis(qkv_sum, 0, 1).reshape(-1, 3 * D),
        out_sum,
        small_sum[1],
        small_sum[2:].T,
        jnp.moveaxis(shared_gu_sum, 0, 1).reshape(-1, 2 * FF),
        shared_down_sum,
        expert_gu_sum,
        expert_down_sum.reshape(held, -1, D).astype(f32),
    )


def solution(mesh):
    rows = P(AX, None)
    split = P("expert", "dp", None)
    in_specs = (rows,) * 4 + (P(AX), rows, rows, P(AX)) + (rows,) * 3 + (split,) * 2
    out_specs = (rows, rows, P(AX), rows, rows, P(AX)) + (rows,) * 3 + (split,) * 2
    inner = functools.partial(body, mesh.shape["dp"], mesh.shape["expert"])
    return jax.shard_map(inner, mesh=mesh, in_specs=in_specs, out_specs=out_specs, check_vma=False)
```
